512 devices in a mesh: grp: 32 (over z, core), vocab: 16 (over x, y).
Axes of the slice: x: 4, y: 4, z: 16, core: 2. Of those that a mesh axis runs over, the one named last changes fastest.
Arguments:
- student_hidden: bfloat16 [512, 5120], P('grp', 'vocab'), may hold values from -120 to 120
- teacher_hidden: bfloat16 [768, 5120], P('grp', 'vocab'), may hold values from -120 to 120
- student_head: bfloat16 [77824, 5120], P(('grp', 'vocab')), may hold values from -0.5 to 0.5
- teacher_head: bfloat16 [77824, 5120], P(('grp', 'vocab')), may hold values from -0.5 to 0.5
- route: int32 [32, 3], replicated, may hold values from 0 to 64, as said below
Outputs:
- head_grad: bfloat16 [77824, 5120], P(('grp', 'vocab'))
- token_kl: float32 [512], P('grp')
The draws below stay inside these ranges and needn't reach their ends.
Inputs may be any that keep to these rules, and one draw needn't show every extreme that they name: route[g, b] is the student block held by slot block b of teacher group g, or 64 for an empty slot; every student block is held exactly once; student block 2 s is held by teacher group s and block 2 s + 1 by teacher group s - 1 or s + 1 (cyclically); a teacher group holds 1 to 3 blocks.
All inputs are finite; a program needn't handle non-finite values.
Results may differ from the reference program's by a relative error of at most 0.015.
Values may be sent and summed in bfloat16 or wider, within the bound.
No kernel may reach another device: no remote copies, remote signals or barrier semaphores. Data moves between devices by JAX's collectives and lax.ppermute only.
A program may use at most 64 MiB of HBM per device.

```python
import math
import jax
import jax.numpy as jnp

D = 5120
TASKS = 8
BLK = 8
TOKENS = 512
NBLK = 64
SLOTS = 768
VOCAB = 77824
N_GRP = 32


def head_rows(key, rows, rise):

    def one_row(row):
        row_key = jax.random.fold_in(key, row)
        noise = jnp.clip(jax.random.normal(jax.random.fold_in(row_key, 0), (D,), jnp.float32), -5.0, 5.0)
        level = jax.random.uniform(jax.random.fold_in(row_key, 1), (), jnp.float32)
        scale = 0.3 * jnp.exp(level * math.log(10.0)) * (1.0 + rise * row.astype(jnp.float32) / VOCAB)
        return jnp.clip(noise * scale / math.sqrt(D), -0.5, 0.5)
    return jax.vmap(one_row)(rows)


def row_scales(key, count):
    level = jax.random.uniform(jax.random.fold_in(key, 1), (count,), jnp.float32)
    return jnp.exp(level * math.log(10.0))


def hidden_drawn(key, count):
    noise = jnp.clip(jax.random.normal(jax.random.fold_in(key, 2), (count, D), jnp.float32), -6.0, 6.0)
    return noise * row_scales(key, count)[:, None]


def draw_student_head(key, part):
    rise = 0.0
    return head_rows(jax.random.fold_in(key, 11), jnp.arange(VOCAB, dtype=jnp.int32), rise).astype(jnp.bfloat16)


def draw_teacher_head(key, part):
    rise = 0.0
    return head_rows(jax.random.fold_in(key, 12), jnp.arange(VOCAB, dtype=jnp.int32), rise).astype(jnp.bfloat16)


def draw_student_hidden(key, part):
    key = jax.random.fold_in(key, 21)
    rows = hidden_drawn(key, TOKENS)
    return rows.astype(jnp.bfloat16)


def draw_teacher_hidden(key, part):
    key = jax.random.fold_in(key, 22)
    rows = hidden_drawn(key, SLOTS)
    return rows.astype(jnp.bfloat16)


def draw_route(key, part):
    key = jax.random.fold_in(key, 5)
    coin = jax.random.randint(jax.random.fold_in(key, 1), (N_GRP,), 0, 2)
    heading = (2 * coin - 1).at[0].set(1).at[2].set(-1)
    groups = jnp.arange(N_GRP, dtype=jnp.int32)
    before = (groups - 1) % N_GRP
    after = (groups + 1) % N_GRP
    own_block = 2 * groups
    from_before = jnp.where(heading[before] == 1, 2 * before + 1, NBLK)
    from_after = jnp.where(heading[after] == -1, 2 * after + 1, NBLK)
    candidates = jnp.stack([own_block, from_before, from_after], axis=1).astype(jnp.int32)
    offsets = jnp.arange(3, dtype=jnp.int32)[None, :]
    scores = jax.random.randint(jax.random.fold_in(key, 2), (N_GRP, 3), 0, 1 << 20) * 4 + offsets
    scores = jnp.where(candidates < NBLK, scores, (1 << 24) + offsets)
    order = jnp.argsort(scores, axis=1, stable=True)
    return jnp.take_along_axis(candidates, order, axis=1).astype(jnp.int32)


def setup_inputs(seed: int = 0) -> dict:
    splits = jax.random.split(jax.random.key(seed), 6)
    return {
        "student_hidden": draw_student_hidden(jax.random.fold_in(splits[5], 71), 0),
        "teacher_hidden": draw_teacher_hidden(jax.random.fold_in(splits[5], 71), 0),
        "student_head": draw_student_head(jax.random.fold_in(splits[5], 71), 0),
        "teacher_head": draw_teacher_head(jax.random.fold_in(splits[5], 71), 0),
        "route": draw_route(jax.random.fold_in(splits[5], 71), 0),
    }


def block_sources(route, groups, tasks, block_rows, total_tokens):
    flat_route = route.reshape(-1)
    block_count = 2 * groups
    block_ids = jnp.arange(block_count, dtype=jnp.int32)
    slot_ids = jnp.arange(flat_route.shape[0], dtype=jnp.int32)
    hits = flat_route[None, :] == block_ids[:, None]
    source = jnp.sum(jnp.where(hits, slot_ids[None, :], 0), axis=1).astype(jnp.int32)
    per_task = groups // tasks
    slot_task = (slot_ids // route.shape[1]) // per_task
    task_ids = jnp.arange(tasks, dtype=jnp.int32)
    alive = flat_route < block_count
    task_blocks = jnp.sum(jnp.where((slot_task[None, :] == task_ids[:, None]) & alive[None, :], 1, 0), axis=1).astype(jnp.int32)
    source_task = (source // route.shape[1]) // per_task
    owning = jnp.sum(jnp.where(source_task[:, None] == task_ids[None, :], task_blocks[None, :], 0), axis=1)
    block_weight = total_tokens / (tasks * block_rows * owning.astype(jnp.float32))
    weight = jnp.repeat(block_weight, block_rows)
    return source, weight


def reference(student_hidden, teacher_hidden, student_head, teacher_head, route):
    source, weight = block_sources(route, N_GRP, TASKS, BLK, TOKENS)
    slot_blocks = teacher_hidden.reshape(SLOTS // BLK, BLK, D)
    aligned = jnp.take(slot_blocks, source, axis=0).reshape(TOKENS, D)
    student_logits = jnp.dot(student_head, student_hidden.T, preferred_element_type=jnp.float32)
    teacher_logits = jnp.dot(teacher_head, aligned.T, preferred_element_type=jnp.float32)
    student_top = jnp.max(student_logits, axis=0)
    teacher_top = jnp.max(teacher_logits, axis=0)
    student_lse = student_top + jnp.log(jnp.sum(jnp.exp(student_logits - student_top[None, :]), axis=0))
    teacher_lse = teacher_top + jnp.log(jnp.sum(jnp.exp(teacher_logits - teacher_top[None, :]), axis=0))
    student_prob = jnp.exp(student_logits - student_lse[None, :])
    teacher_prob = jnp.exp(teacher_logits - teacher_lse[None, :])
    token_kl = jnp.sum(teacher_prob * (teacher_logits - student_logits), axis=0) - teacher_lse + student_lse
    logit_grad = (weight[None, :] * (student_prob - teacher_prob)).astype(jnp.bfloat16)
    head_grad = jnp.dot(logit_grad, student_hidden, preferred_element_type=jnp.float32).astype(jnp.bfloat16)
    return (head_grad, token_kl)
```

```python
import jax
import jax.numpy as jnp
import numpy as np
from jax import lax
from jax.sharding import Mesh, PartitionSpec as P

TASKS = 8
NZ, NC, NX, NY = 16, 2, 4, 4
BLK = 8
SWAP = [(0, 1), (1, 0)]


def block_sources(route, groups, tasks, block_rows, total_tokens):
    flat_route = route.reshape(-1)
    block_count = 2 * groups
    block_ids = jnp.arange(block_count, dtype=jnp.int32)
    slot_ids = jnp.arange(flat_route.shape[0], dtype=jnp.int32)
    hits = flat_route[None, :] == block_ids[:, None]
    source = jnp.sum(jnp.where(hits, slot_ids[None, :], 0), axis=1)
    per_task = groups // tasks
    slot_task = slot_ids // route.shape[1] // per_task
    task_ids = jnp.arange(tasks, dtype=jnp.int32)
    alive = flat_route < block_count
    task_blocks = jnp.sum(
        jnp.where((slot_task[None, :] == task_ids[:, None]) & alive[None, :], 1, 0), axis=1
    ).astype(jnp.int32)
    source_task = source // route.shape[1] // per_task
    owning = jnp.sum(
        jnp.where(source_task[:, None] == task_ids[None, :], task_blocks[None, :], 0), axis=1
    )
    block_weight = total_tokens / (tasks * block_rows * owning.astype(jnp.float32))
    return source, block_weight


def spread(x, axes, n):
    return lax.all_to_all(jnp.broadcast_to(x[None], (n,) + x.shape), axes, 0, 0)


def ring_pieces(x, axis, n):
    me = lax.axis_index(axis)
    pieces = [x]
    for shift in range(1, n):
        pieces.append(lax.ppermute(x, axis, [(i, (i + shift) % n) for i in range(n)]))
    out = jnp.zeros((n,) + x.shape, x.dtype)
    for shift, piece in enumerate(pieces):
        out = lax.dynamic_update_index_in_dim(out, piece, (me - shift) % n, 0)
    return out


def merge(stats):
    top = jnp.max(stats[:, 0:2], axis=0)
    scale = jnp.exp(stats[:, 0:2] - top[None])
    total = jnp.sum(stats[:, 2:4] * scale, axis=0)
    cross = jnp.sum(stats[:, 4:5] * scale[:, 0:1], axis=0)
    return jnp.concatenate([top, total, cross, jnp.zeros((3, top.shape[1]), top.dtype)], axis=0)


def per_device(student_hidden, teacher_hidden, student_head, teacher_head, route):
    core = lax.axis_index("core")
    z = lax.axis_index("z")
    feats = student_hidden.shape[1]
    rows = student_head.shape[0]
    groups = NZ * NC
    half = NZ * BLK
    cols = 2 * half
    width = NX * NY * feats

    student_other = lax.ppermute(student_head, "core", SWAP)
    teacher_other = lax.ppermute(teacher_head, "core", SWAP)

    source, block_weight = block_sources(route, groups, TASKS, BLK, groups * 2 * BLK)
    zs = jnp.arange(NZ, dtype=jnp.int32)
    blocks = jnp.concatenate([2 * (2 * zs + core), 2 * (2 * zs + 1 - core) + 1])
    my_source = jnp.take(source, blocks)
    my_weight = jnp.repeat(jnp.take(block_weight, blocks), BLK)

    odd = lax.all_gather(student_hidden[BLK:], "core")
    odd = lax.dynamic_index_in_dim(odd, 1 - core, 0, keepdims=False)
    held = jnp.concatenate([student_hidden[:BLK], odd, teacher_hidden], axis=0)
    n_rows = held.shape[0]
    packed = jnp.concatenate(
        [
            held[:, :128],
            held[:, 128:256],
            jnp.concatenate([held[: n_rows // 2, 256:], held[n_rows // 2 :, 256:]], axis=1),
        ],
        axis=0,
    )
    got = spread(packed, "z", NZ)
    tail = got[:, 2 * n_rows :]
    slots = jnp.concatenate(
        [
            got[:, :n_rows],
            got[:, n_rows : 2 * n_rows],
            jnp.concatenate([tail[:, :, :64], tail[:, :, 64:]], axis=1),
        ],
        axis=2,
    ).reshape(NZ * n_rows, feats)
    inner = jnp.arange(BLK, dtype=jnp.int32)
    s_rows = (
        zs[None, :, None] * n_rows
        + jnp.arange(2, dtype=jnp.int32)[:, None, None] * BLK
        + inner[None, None, :]
    ).reshape(-1)
    t_first = (my_source // 3 // 2) * n_rows + 2 * BLK + (my_source % 3) * BLK
    t_rows = (t_first[:, None] + inner[None, :]).reshape(-1)
    pick = jnp.concatenate([s_rows, t_rows])
    onehot = (
        jnp.arange(NZ * n_rows, dtype=jnp.int32)[:, None] == pick[None, :]
    ).astype(jnp.bfloat16)
    placed = lax.dot_general(
        slots, onehot, (((0,), (0,)), ((), ())), preferred_element_type=jnp.float32
    ).astype(jnp.bfloat16)

    student_y = spread(placed[:, :cols], "y", NY)
    teacher_x = ring_pieces(placed[:, cols:], "x", NX)
    student_y, teacher_x = lax.optimization_barrier((student_y, teacher_x))
    student_t = spread(student_y, "x", NX).reshape(width, cols)
    teacher_yx = ring_pieces(teacher_x, "y", NY)
    teacher_t = jnp.swapaxes(teacher_yx, 0, 1).reshape(width, cols)

    student_partner = lax.ppermute(student_t, "core", SWAP)

    head_s = jnp.concatenate([student_head, student_other], axis=0)
    head_t = jnp.concatenate([teacher_head, teacher_other], axis=0)
    ls = jnp.dot(head_s, student_t, preferred_element_type=jnp.float32)
    lt = jnp.dot(head_t, teacher_t, preferred_element_type=jnp.float32)
    ms = jnp.max(ls, axis=0)
    mt = jnp.max(lt, axis=0)
    es = jnp.exp(ls - ms[None])
    et = jnp.exp(lt - mt[None])
    zero = jnp.zeros_like(ms)
    stats = jnp.stack(
        [mt, ms, jnp.sum(et, axis=0), jnp.sum(es, axis=0), jnp.sum(et * (lt - ls), axis=0), zero, zero, zero]
    )
    stats = merge(spread(stats, ("x", "y"), NX * NY))
    stats = merge(spread(stats, "z", NZ))
    lse = stats[0:2] + jnp.log(stats[2:4])
    token_loss = stats[4] / stats[2] - lse[0] + lse[1]
    grad = (
        my_weight[None] * (jnp.exp(ls - lse[1][None]) - jnp.exp(lt - lse[0][None]))
    ).astype(jnp.bfloat16)

    grad_in = lax.all_gather(grad[rows:], "core")
    grad_in = lax.dynamic_index_in_dim(grad_in, 1 - core, 0, keepdims=False)
    nt = (((1,), (1,)), ((), ()))
    head_grad = lax.dot_general(
        jnp.concatenate([grad[:rows], grad_in], axis=1),
        jnp.concatenate([student_t, student_partner], axis=1),
        nt,
        preferred_element_type=jnp.float32,
    ).astype(jnp.bfloat16)

    odd_loss = lax.all_gather(token_loss[half:], "core")
    odd_loss = lax.dynamic_index_in_dim(odd_loss, 1 - core, 0, keepdims=False)
    own_loss = jnp.concatenate(
        [
            lax.dynamic_slice_in_dim(token_loss, z * BLK, BLK, 0),
            lax.dynamic_slice_in_dim(odd_loss, z * BLK, BLK, 0),
        ]
    )
    return head_grad, own_loss


def solution(mesh):
    mesh = Mesh(np.asarray(mesh.devices).reshape(NZ, NC, NX, NY), ("z", "core", "x", "y"))
    grp, voc = ("z", "core"), ("x", "y")
    return jax.shard_map(
        per_device,
        mesh=mesh,
        in_specs=(P(grp, voc), P(grp, voc), P(grp + voc, None), P(grp + voc, None), P()),
        out_specs=(P(grp + voc, None), P(grp)),
        check_vma=False,
    )
```

```python
import functools

import jax
import jax.numpy as jnp
import numpy as np
from jax import lax
from jax.experimental import pallas as pl
from jax.experimental.pallas import tpu as pltpu
from jax.sharding import Mesh, PartitionSpec as P

TASKS = 8
NZ, NC, NX, NY = 16, 2, 4, 4
BLK = 8
SWAP = [(0, 1), (1, 0)]


def block_sources(route, groups, tasks, block_rows, total_tokens):
    flat_route = route.reshape(-1)
    block_count = 2 * groups
    block_ids = jnp.arange(block_count, dtype=jnp.int32)
    slot_ids = jnp.arange(flat_route.shape[0], dtype=jnp.int32)
    hits = flat_route[None, :] == block_ids[:, None]
    source = jnp.sum(jnp.where(hits, slot_ids[None, :], 0), axis=1)
    per_task = groups // tasks
    slot_task = slot_ids // route.shape[1] // per_task
    task_ids = jnp.arange(tasks, dtype=jnp.int32)
    alive = flat_route < block_count
    task_blocks = jnp.sum(
        jnp.where((slot_task[None, :] == task_ids[:, None]) & alive[None, :], 1, 0), axis=1
    ).astype(jnp.int32)
    source_task = source // route.shape[1] // per_task
    owning = jnp.sum(
        jnp.where(source_task[:, None] == task_ids[None, :], task_blocks[None, :], 0), axis=1
    )
    block_weight = total_tokens / (tasks * block_rows * owning.astype(jnp.float32))
    return source, block_weight


def spread(x, axes, n):
    return lax.all_to_all(jnp.broadcast_to(x[None], (n,) + x.shape), axes, 0, 0)


def merge(stats, t):
    top = jnp.max(stats[:, :, : 2 * t], axis=0)
    scale = jnp.exp(stats[:, :, : 2 * t] - top[None])
    total = jnp.sum(stats[:, :, 2 * t : 4 * t] * scale, axis=0)
    cross = jnp.sum(stats[:, :, 4 * t :] * scale[:, :, :t], axis=0)
    return jnp.concatenate([top, total, cross], axis=1)


LINES_X = [[x * NY + y for x in range(NX)] for y in range(NY)]
LINES_Y = [[x * NY + y for y in range(NY)] for x in range(NX)]


def by_core(first, second):
    return first + [[NX * NY + i for i in line] for line in second]


FIRST, LAST = by_core(LINES_X, LINES_Y), by_core(LINES_Y, LINES_X)


def spread_groups(x, axes, lines):
    copies = jnp.broadcast_to(x[None], (len(lines[0]),) + x.shape)
    return lax.all_to_all(copies, axes, 0, 0, axis_index_groups=lines)


def place_kernel(n, shifts, *refs):
    pieces, outs = refs[: 2 * n], refs[-2:]
    core = lax.axis_index("core")
    me = jnp.where(core == 0, lax.axis_index("y"), lax.axis_index("x"))
    for i, piece in enumerate(pieces):
        source = (me - shifts[i % n]) & (NX - 1)
        for j in range(NX):
            a = jnp.where(core == 0, j, source)
            b = jnp.where(core == 0, source, j)
            outs[i // n][a, b] = piece[j]


def place(pieces, shifts, shape, into=()):
    n = len(shifts)
    whole = pl.BlockSpec(memory_space=pltpu.VMEM)
    return pl.pallas_call(
        functools.partial(place_kernel, n, shifts),
        out_shape=(jax.ShapeDtypeStruct(shape, pieces[0].dtype),) * 2,
        in_specs=[whole] * (2 * n + len(into)),
        out_specs=(whole,) * 2,
        input_output_aliases={2 * n + i: i for i in range(len(into))},
        compiler_params=pltpu.CompilerParams(vmem_limit_bytes=20 * 1024 * 1024),
        name="place_blocks",
    )(*pieces, *(pltpu.with_memory_space_constraint(b, pltpu.VMEM) for b in into))


def per_device(student_hidden, teacher_hidden, student_head, teacher_head, route):
    core = lax.axis_index("core")
    x, y, z = lax.axis_index("x"), lax.axis_index("y"), lax.axis_index("z")
    feats = student_hidden.shape[1]
    rows = student_head.shape[0]
    groups = NZ * NC
    per_group = 2 * BLK
    half = NZ * BLK
    cols = 2 * half
    width = NX * NY * feats
    f32, bf16 = jnp.float32, jnp.bfloat16

    held = jnp.concatenate([student_hidden, teacher_hidden], axis=0)
    n_rows = held.shape[0]
    got = lax.all_gather(held, ("z", "core"))
    row = lax.broadcasted_iota(jnp.int32, (groups, n_rows), 1)
    group = lax.broadcasted_iota(jnp.int32, (groups, n_rows), 0)
    block = 2 * group + row // BLK
    for b in range(route.shape[1]):
        block = jnp.where((row - per_group) // BLK == b, route[:, b : b + 1], block)
    column = (block & 1) * half + (block >> 2) * BLK + row % BLK + jnp.where(row < per_group, 0, cols)
    mine = (block < 2 * groups) & (((block >> 1) & 1) == core)
    column = jnp.where(mine, column, -1)
    onehot = (column[:, :, None] == jnp.arange(2 * cols, dtype=jnp.int32)).astype(bf16)
    placed = lax.dot_general(
        got, onehot, (((0, 1), (0, 1)), ((), ())), preferred_element_type=f32
    ).astype(bf16)

    student_other = lax.ppermute(student_head, "core", SWAP)
    teacher_other = lax.ppermute(teacher_head, "core", SWAP)

    plane = ("core", "x", "y")
    both = jnp.stack([placed[:, :cols], placed[:, cols:]])
    once = spread_groups(both, plane, FIRST)
    student_1, teacher_1 = once[:, 0], once[:, 1]

    def pass_on(piece, k):
        return lax.ppermute(piece, plane, [(i[j], i[(j + k) % len(i)]) for i in LAST for j in range(len(i))])

    student_b, teacher_a = pass_on(student_1, 1), pass_on(teacher_1, 3)
    student_a, teacher_b = pass_on(student_1, 3), pass_on(teacher_1, 1)
    student_b, teacher_a, student_other, teacher_other = lax.optimization_barrier(
        (student_b, teacher_a, student_other, teacher_other)
    )
    student_c, teacher_c = pass_on(student_b, 1), pass_on(teacher_a, 3)
    shape = (NX, NY, feats, cols)
    student_t, teacher_t = place(
        (student_1, student_b, student_a, student_c, teacher_1, teacher_b, teacher_a, teacher_c),
        (0, 1, 3, 2),
        shape,
    )
    student_t, teacher_t = student_t.reshape(width, cols), teacher_t.reshape(width, cols)

    head_s = jnp.concatenate([student_head, student_other], axis=0)
    head_t = jnp.concatenate([teacher_head, teacher_other], axis=0)
    ls = jnp.dot(head_s, student_t, preferred_element_type=f32)
    lt = jnp.dot(head_t, teacher_t, preferred_element_type=f32)
    source, block_weight = block_sources(route, groups, TASKS, BLK, groups * per_group)
    my_weight = lax.dynamic_index_in_dim(block_weight.reshape(NZ, NC, 2), core, 1, keepdims=False)
    my_weight = jnp.repeat(my_weight.T.reshape(-1), BLK)
    ms = jnp.max(ls, axis=0)
    mt = jnp.max(lt, axis=0)
    es = jnp.exp(ls - ms[None])
    et = jnp.exp(lt - mt[None])
    stats = jnp.concatenate(
        [mt, ms, jnp.sum(et, axis=0), jnp.sum(es, axis=0), jnp.sum(et * (lt - ls), axis=0)]
    )[None]
    stats = merge(spread(stats, ("x", "y"), NX * NY), cols)
    stats, student_t = lax.optimization_barrier((stats, student_t))
    student_mate = lax.ppermute(student_t, "core", SWAP)
    stats = merge(spread(stats, "z", NZ), cols)[0]
    top_t, top_s, sum_t, sum_s = (stats[i * cols : (i + 1) * cols] for i in range(4))
    lse_t = top_t + jnp.log(sum_t)
    lse_s = top_s + jnp.log(sum_s)
    grad = (
        my_weight[None] * (jnp.exp(ls - lse_s[None]) - jnp.exp(lt - lse_t[None]))
    ).astype(bf16)

    grad_in = lax.all_gather(grad[rows:], "core")
    grad_in = lax.dynamic_index_in_dim(grad_in, 1 - core, 0, keepdims=False)
    nt = (((1,), (1,)), ((), ()))
    head_grad = lax.dot_general(
        jnp.concatenate([grad[:rows], grad_in], axis=1),
        jnp.concatenate([student_t, student_mate], axis=1),
        nt,
        preferred_element_type=f32,
    ).astype(bf16)
    own = lax.dynamic_index_in_dim(stats.reshape(10, NZ, BLK), z, 1, keepdims=False)
    own = own.reshape(5, per_group)
    loss = own[4] / own[2] - (own[0] + jnp.log(own[2])) + (own[1] + jnp.log(own[3]))
    return head_grad, loss


def solution(mesh):
    mesh = Mesh(np.asarray(mesh.devices).reshape(NZ, NC, NX, NY), ("z", "core", "x", "y"))
    grp, voc = ("z", "core"), ("x", "y")
    return jax.shard_map(
        per_device,
        mesh=mesh,
        in_specs=(P(grp, voc), P(grp, voc), P(grp + voc, None), P(grp + voc, None), P()),
        out_specs=(P(grp + voc, None), P(grp)),
        check_vma=False,
    )
```

```python
import functools

import jax
import jax.numpy as jnp
import numpy as np
from jax import lax
from jax.experimental import pallas as pl
from jax.experimental.pallas import tpu as pltpu
from jax.sharding import Mesh, PartitionSpec as P

TASKS = 8
NZ, NC, NX, NY = 16, 2, 4, 4
BLK = 8
SWAP = [(0, 1), (1, 0)]


def block_sources(route, groups, tasks, block_rows, total_tokens):
    flat_route = route.reshape(-1)
    block_count = 2 * groups
    block_ids = jnp.arange(block_count, dtype=jnp.int32)
    slot_ids = jnp.arange(flat_route.shape[0], dtype=jnp.int32)
    hits = flat_route[None, :] == block_ids[:, None]
    source = jnp.sum(jnp.where(hits, slot_ids[None, :], 0), axis=1)
    per_task = groups // tasks
    slot_task = slot_ids // route.shape[1] // per_task
    task_ids = jnp.arange(tasks, dtype=jnp.int32)
    alive = flat_route < block_count
    task_blocks = jnp.sum(
        jnp.where((slot_task[None, :] == task_ids[:, None]) & alive[None, :], 1, 0), axis=1
    ).astype(jnp.int32)
    source_task = source // route.shape[1] // per_task
    owning = jnp.sum(
        jnp.where(source_task[:, None] == task_ids[None, :], task_blocks[None, :], 0), axis=1
    )
    block_weight = total_tokens / (tasks * block_rows * owning.astype(jnp.float32))
    return source, block_weight


def spread(x, axes, n):
    return lax.all_to_all(jnp.broadcast_to(x[None], (n,) + x.shape), axes, 0, 0)


def merge(stats, t):
    top = jnp.max(stats[:, :, : 2 * t], axis=0)
    scale = jnp.exp(stats[:, :, : 2 * t] - top[None])
    total = jnp.sum(scale, axis=0)
    mean = jnp.sum(stats[:, :, 2 * t :] * scale[:, :, :t], axis=0) / total[:, :t]
    return jnp.concatenate([top + jnp.log(total), mean], axis=1)


LINES_X = [[x * NY + y for x in range(NX)] for y in range(NY)]
LINES_Y = [[x * NY + y for y in range(NY)] for x in range(NX)]


def by_core(first, second):
    return first + [[NX * NY + i for i in line] for line in second]


FIRST, LAST = by_core(LINES_X, LINES_Y), by_core(LINES_Y, LINES_X)


def spread_groups(x, axes, lines):
    copies = jnp.broadcast_to(x[None], (len(lines[0]),) + x.shape)
    return lax.all_to_all(copies, axes, 0, 0, axis_index_groups=lines)


def place_kernel(shifts, *refs):
    out = refs[-1]
    core = lax.axis_index("core")
    me = jnp.where(core == 0, lax.axis_index("y"), lax.axis_index("x"))
    for piece, shift in zip(refs, shifts):
        source = (me - shift) & (NX - 1)
        for j in range(NX):
            a = jnp.where(core == 0, j, source)
            b = jnp.where(core == 0, source, j)
            out[a, b] = piece[j]


def place(pieces, shifts, into=()):
    n = len(pieces)
    whole = pl.BlockSpec(memory_space=pltpu.VMEM)
    shape = (NX, NY) + pieces[0].shape[1:]
    return pl.pallas_call(
        functools.partial(place_kernel, shifts),
        out_shape=jax.ShapeDtypeStruct(shape, pieces[0].dtype),
        in_specs=[whole] * (n + len(into)),
        out_specs=whole,
        input_output_aliases={n: 0} if into else {},
        compiler_params=pltpu.CompilerParams(vmem_limit_bytes=8 * 1024 * 1024),
        name="place_blocks",
    )(*pieces, *(pltpu.with_memory_space_constraint(b, pltpu.VMEM) for b in into))


def per_device(student_hidden, teacher_hidden, student_head, teacher_head, route):
    core = lax.axis_index("core")
    x, y, z = lax.axis_index("x"), lax.axis_index("y"), lax.axis_index("z")
    feats = student_hidden.shape[1]
    rows = student_head.shape[0]
    groups = NZ * NC
    per_group = 2 * BLK
    half = NZ * BLK
    cols = 2 * half
    width = NX * NY * feats
    f32, bf16 = jnp.float32, jnp.bfloat16

    held = jnp.concatenate([student_hidden, teacher_hidden], axis=0)
    n_rows = held.shape[0]
    got = lax.all_gather(held, ("z", "core"))
    row = lax.broadcasted_iota(jnp.int32, (groups, n_rows), 1)
    group = lax.broadcasted_iota(jnp.int32, (groups, n_rows), 0)
    block = 2 * group + row // BLK
    for b in range(route.shape[1]):
        block = jnp.where((row - per_group) // BLK == b, route[:, b : b + 1], block)
    column = (block & 1) * half + (block >> 2) * BLK + row % BLK + jnp.where(row < per_group, 0, cols)
    mine = (block < 2 * groups) & (((block >> 1) & 1) == core)
    column = jnp.where(mine, column, -1)
    onehot = (column[:, :, None] == jnp.arange(2 * cols, dtype=jnp.int32)).astype(bf16)
    placed = lax.dot_general(
        got, onehot, (((0, 1), (0, 1)), ((), ())), preferred_element_type=f32
    ).astype(bf16)

    student_other = lax.ppermute(student_head, "core", SWAP)
    teacher_other = lax.ppermute(teacher_head, "core", SWAP)

    plane = ("core", "x", "y")
    both = jnp.stack([placed[:, :cols], placed[:, cols:]])
    once = spread_groups(both, plane, FIRST)
    student_1, teacher_1 = once[:, 0], once[:, 1]

    def pass_on(piece, k):
        return lax.ppermute(piece, plane, [(i[j], i[(j + k) % len(i)]) for i in LAST for j in range(len(i))])

    student_b, teacher_a = pass_on(student_1, 1), pass_on(teacher_1, 3)
    student_a, teacher_b = pass_on(student_1, 3), pass_on(teacher_1, 1)
    student_b, teacher_a, student_other, teacher_other = lax.optimization_barrier(
        (student_b, teacher_a, student_other, teacher_other)
    )
    student_c, teacher_c = pass_on(student_b, 1), pass_on(teacher_a, 3)
    near_s = place((student_1, student_b, student_a), (0, 1, 3))
    near_t = place((teacher_1, teacher_b, teacher_a), (0, 1, 3))
    student_t = place((student_c,), (2,), (near_s,)).reshape(width, cols)
    teacher_t = place((teacher_c,), (2,), (near_t,)).reshape(width, cols)

    student_mate = lax.ppermute(student_t, "core", SWAP)

    head_s = jnp.concatenate([student_head, student_other], axis=0)
    head_t = jnp.concatenate([teacher_head, teacher_other], axis=0)
    ls = jnp.dot(head_s, student_t, preferred_element_type=f32)
    lt = jnp.dot(head_t, teacher_t, preferred_element_type=f32)
    source, block_weight = block_sources(route, groups, TASKS, BLK, groups * per_group)
    my_weight = lax.dynamic_index_in_dim(block_weight.reshape(NZ, NC, 2), core, 1, keepdims=False)
    my_weight = jnp.repeat(my_weight.T.reshape(-1), BLK)
    ms = jnp.max(ls, axis=0)
    mt = jnp.max(lt, axis=0)
    es = jnp.exp(ls - ms[None])
    et = jnp.exp(lt - mt[None])
    total_s, total_t = jnp.sum(es, axis=0), jnp.sum(et, axis=0)
    mean = jnp.sum(et * (lt - ls), axis=0) / total_t
    stats = jnp.concatenate([mt + jnp.log(total_t), ms + jnp.log(total_s), mean])[None]
    stats = merge(spread(stats, ("x", "y"), NX * NY), cols)
    stats = merge(spread(stats, "z", NZ), cols)[0]
    lse_t, lse_s = stats[:cols], stats[cols : 2 * cols]
    grad = (
        my_weight[None] * (jnp.exp(ls - lse_s[None]) - jnp.exp(lt - lse_t[None]))
    ).astype(bf16)

    grad_in = lax.all_gather(grad[rows:], "core")
    grad_in = lax.dynamic_index_in_dim(grad_in, 1 - core, 0, keepdims=False)
    nt = (((1,), (1,)), ((), ()))
    head_grad = lax.dot_general(
        jnp.concatenate([grad[:rows], grad_in], axis=1),
        jnp.concatenate([student_t, student_mate], axis=1),
        nt,
        preferred_element_type=f32,
    ).astype(bf16)
    own = lax.dynamic_index_in_dim(stats.reshape(6, NZ, BLK), z, 1, keepdims=False)
    own = own.reshape(3, per_group)
    loss = own[2] - own[0] + own[1]
    return head_grad, loss


def solution(mesh):
    mesh = Mesh(np.asarray(mesh.devices).reshape(NZ, NC, NX, NY), ("z", "core", "x", "y"))
    grp, voc = ("z", "core"), ("x", "y")
    return jax.shard_map(
        per_device,
        mesh=mesh,
        in_specs=(P(grp, voc), P(grp, voc), P(grp + voc, None), P(grp + voc, None), P()),
        out_specs=(P(grp + voc, None), P(grp)),
        check_vma=False,
    )
```

```python
import functools

import jax
import jax.numpy as jnp
import numpy as np
from jax import lax
from jax.experimental import pallas as pl
from jax.experimental.pallas import tpu as pltpu
from jax.sharding import Mesh, PartitionSpec as P

TASKS = 8
NZ, NC, NX, NY = 16, 2, 4, 4
BLK = 8
SWAP = [(0, 1), (1, 0)]


def block_sources(route, groups, tasks, block_rows, total_tokens):
    flat_route = route.reshape(-1)
    block_count = 2 * groups
    block_ids = jnp.arange(block_count, dtype=jnp.int32)
    slot_ids = jnp.arange(flat_route.shape[0], dtype=jnp.int32)
    hits = flat_route[None, :] == block_ids[:, None]
    source = jnp.sum(jnp.where(hits, slot_ids[None, :], 0), axis=1)
    per_task = groups // tasks
    slot_task = slot_ids // route.shape[1] // per_task
    task_ids = jnp.arange(tasks, dtype=jnp.int32)
    alive = flat_route < block_count
    task_blocks = jnp.sum(
        jnp.where((slot_task[None, :] == task_ids[:, None]) & alive[None, :], 1, 0), axis=1
    ).astype(jnp.int32)
    source_task = source // route.shape[1] // per_task
    owning = jnp.sum(
        jnp.where(source_task[:, None] == task_ids[None, :], task_blocks[None, :], 0), axis=1
    )
    block_weight = total_tokens / (tasks * block_rows * owning.astype(jnp.float32))
    return source, block_weight


def spread(x, axes, n):
    return lax.all_to_all(jnp.broadcast_to(x[None], (n,) + x.shape), axes, 0, 0)


def merge(stats, t):
    top = jnp.max(stats[:, :, : 2 * t], axis=0)
    scale = jnp.exp(stats[:, :, : 2 * t] - top[None])
    total = jnp.sum(scale, axis=0)
    mean = jnp.sum(stats[:, :, 2 * t :] * scale[:, :, :t], axis=0) / total[:, :t]
    return jnp.concatenate([top + jnp.log(total), mean], axis=1)


LINES_X = [[x * NY + y for x in range(NX)] for y in range(NY)]
LINES_Y = [[x * NY + y for y in range(NY)] for x in range(NX)]


def by_core(first, second):
    return first + [[NX * NY + i for i in line] for line in second]


FIRST, LAST = by_core(LINES_X, LINES_Y), by_core(LINES_Y, LINES_X)


def spread_groups(x, axes, lines):
    copies = jnp.broadcast_to(x[None], (len(lines[0]),) + x.shape)
    return lax.all_to_all(copies, axes, 0, 0, axis_index_groups=lines)


def place_kernel(shifts, *refs):
    out = refs[-1]
    core = lax.axis_index("core")
    me = jnp.where(core == 0, lax.axis_index("y"), lax.axis_index("x"))
    for piece, shift in zip(refs, shifts):
        source = (me - shift) & (NX - 1)
        for j in range(NX):
            a = jnp.where(core == 0, j, source)
            b = jnp.where(core == 0, source, j)
            out[a, b] = piece[j]


def place(pieces, shifts, into=()):
    n = len(pieces)
    whole = pl.BlockSpec(memory_space=pltpu.VMEM)
    shape = (NX, NY) + pieces[0].shape[1:]
    return pl.pallas_call(
        functools.partial(place_kernel, shifts),
        out_shape=jax.ShapeDtypeStruct(shape, pieces[0].dtype),
        in_specs=[whole] * (n + len(into)),
        out_specs=whole,
        input_output_aliases={n: 0} if into else {},
        compiler_params=pltpu.CompilerParams(vmem_limit_bytes=8 * 1024 * 1024),
        name="place_blocks",
    )(*pieces, *(pltpu.with_memory_space_constraint(b, pltpu.VMEM) for b in into))


def per_device(student_hidden, teacher_hidden, student_head, teacher_head, route):
    core = lax.axis_index("core")
    x, y, z = lax.axis_index("x"), lax.axis_index("y"), lax.axis_index("z")
    feats = student_hidden.shape[1]
    rows = student_head.shape[0]
    groups = NZ * NC
    per_group = 2 * BLK
    half = NZ * BLK
    cols = 2 * half
    width = NX * NY * feats
    f32, bf16 = jnp.float32, jnp.bfloat16

    held = jnp.concatenate([student_hidden, teacher_hidden], axis=0)
    n_rows = held.shape[0]
    got = lax.all_gather(held, ("z", "core"))
    row = lax.broadcasted_iota(jnp.int32, (groups, n_rows), 1)
    group = lax.broadcasted_iota(jnp.int32, (groups, n_rows), 0)
    block = 2 * group + row // BLK
    for b in range(route.shape[1]):
        block = jnp.where((row - per_group) // BLK == b, route[:, b : b + 1], block)
    column = (block & 1) * half + (block >> 2) * BLK + row % BLK + jnp.where(row < per_group, 0, cols)
    mine = (block < 2 * groups) & (((block >> 1) & 1) == core)
    column = jnp.where(mine, column, -1)
    onehot = (column[:, :, None] == jnp.arange(2 * cols, dtype=jnp.int32)).astype(bf16)
    placed = lax.dot_general(
        got, onehot, (((0, 1), (0, 1)), ((), ())), preferred_element_type=f32
    ).astype(bf16)

    student_other = lax.ppermute(student_head, "core", SWAP)
    teacher_other = lax.ppermute(teacher_head, "core", SWAP)

    plane = ("core", "x", "y")
    both = jnp.stack([placed[:, :cols], placed[:, cols:]])
    once = spread_groups(both, plane, FIRST)
    student_1, teacher_1 = once[:, 0], once[:, 1]

    def pass_on(piece, k):
        return lax.ppermute(piece, plane, [(i[j], i[(j + k) % len(i)]) for i in LAST for j in range(len(i))])

    student_b, teacher_a = pass_on(student_1, 1), pass_on(teacher_1, 3)
    student_a, teacher_b = pass_on(student_1, 3), pass_on(teacher_1, 1)
    student_b, student_other = lax.optimization_barrier((student_b, student_other))
    teacher_a, teacher_other = lax.optimization_barrier((teacher_a, teacher_other))
    student_c, teacher_c = pass_on(student_b, 1), pass_on(teacher_a, 3)
    near_s = place((student_1, student_b, student_a), (0, 1, 3))
    near_t = place((teacher_1, teacher_b, teacher_a), (0, 1, 3))
    head_s = jnp.concatenate([student_head, student_other], axis=0)
    head_t = jnp.concatenate([teacher_head, teacher_other], axis=0)
    near_s, head_s = lax.optimization_barrier((near_s, head_s))
    near_t, head_t = lax.optimization_barrier((near_t, head_t))
    student_t = place((student_c,), (2,), (near_s,)).reshape(width, cols)
    teacher_t = place((teacher_c,), (2,), (near_t,)).reshape(width, cols)

    student_mate = lax.ppermute(student_t, "core", SWAP)

    ls = jnp.dot(head_s, student_t, preferred_element_type=f32)
    lt = jnp.dot(head_t, teacher_t, preferred_element_type=f32)
    source, block_weight = block_sources(route, groups, TASKS, BLK, groups * per_group)
    my_weight = lax.dynamic_index_in_dim(block_weight.reshape(NZ, NC, 2), core, 1, keepdims=False)
    my_weight = jnp.repeat(my_weight.T.reshape(-1), BLK)
    ms = jnp.max(ls, axis=0)
    mt = jnp.max(lt, axis=0)
    es = jnp.exp(ls - ms[None])
    et = jnp.exp(lt - mt[None])
    total_s, total_t = jnp.sum(es, axis=0), jnp.sum(et, axis=0)
    mean = jnp.sum(et * (lt - ls), axis=0) / total_t
    stats = jnp.concatenate([mt + jnp.log(total_t), ms + jnp.log(total_s), mean])[None]
    stats = merge(spread(stats, ("x", "y"), NX * NY), cols)
    stats = merge(spread(stats, "z", NZ), cols)[0]
    lse_t, lse_s = stats[:cols], stats[cols : 2 * cols]
    grad = (
        my_weight[None] * (jnp.exp(ls - lse_s[None]) - jnp.exp(lt - lse_t[None]))
    ).astype(bf16)

    grad_in = lax.all_gather(grad[rows:], "core")
    grad_in = lax.dynamic_index_in_dim(grad_in, 1 - core, 0, keepdims=False)
    nt = (((1,), (1,)), ((), ()))
    head_grad = lax.dot_general(
        jnp.concatenate([grad[:rows], grad_in], axis=1),
        jnp.concatenate([student_t, student_mate], axis=1),
        nt,
        preferred_element_type=f32,
    ).astype(bf16)
    own = lax.dynamic_index_in_dim(stats.reshape(6, NZ, BLK), z, 1, keepdims=False)
    own = own.reshape(3, per_group)
    loss = own[2] - own[0] + own[1]
    return head_grad, loss


def solution(mesh):
    mesh = Mesh(np.asarray(mesh.devices).reshape(NZ, NC, NX, NY), ("z", "core", "x", "y"))
    grp, voc = ("z", "core"), ("x", "y")
    return jax.shard_map(
        per_device,
        mesh=mesh,
        in_specs=(P(grp, voc), P(grp, voc), P(grp + voc, None), P(grp + voc, None), P()),
        out_specs=(P(grp + voc, None), P(grp)),
        check_vma=False,
    )
```

```python
import functools

import jax
import jax.numpy as jnp
import numpy as np
from jax import lax
from jax.experimental import pallas as pl
from jax.experimental.pallas import tpu as pltpu
from jax.sharding import Mesh, PartitionSpec as P

TASKS = 8
NZ, NC, NX, NY = 16, 2, 4, 4
BLK = 8
SWAP = [(0, 1), (1, 0)]


def block_sources(route, groups, tasks, block_rows, total_tokens):
    flat_route = route.reshape(-1)
    block_count = 2 * groups
    block_ids = jnp.arange(block_count, dtype=jnp.int32)
    slot_ids = jnp.arange(flat_route.shape[0], dtype=jnp.int32)
    hits = flat_route[None, :] == block_ids[:, None]
    source = jnp.sum(jnp.where(hits, slot_ids[None, :], 0), axis=1)
    per_task = groups // tasks
    slot_task = slot_ids // route.shape[1] // per_task
    task_ids = jnp.arange(tasks, dtype=jnp.int32)
    alive = flat_route < block_count
    task_blocks = jnp.sum(
        jnp.where((slot_task[None, :] == task_ids[:, None]) & alive[None, :], 1, 0), axis=1
    ).astype(jnp.int32)
    source_task = source // route.shape[1] // per_task
    owning = jnp.sum(
        jnp.where(source_task[:, None] == task_ids[None, :], task_blocks[None, :], 0), axis=1
    )
    block_weight = total_tokens / (tasks * block_rows * owning.astype(jnp.float32))
    return source, block_weight


def spread(x, axes, n):
    return lax.all_to_all(jnp.broadcast_to(x[None], (n,) + x.shape), axes, 0, 0)


def merge(stats, t):
    top = jnp.max(stats[:, :, : 2 * t], axis=0)
    scale = jnp.exp(stats[:, :, : 2 * t] - top[None])
    total = jnp.sum(scale, axis=0)
    mean = jnp.sum(stats[:, :, 2 * t :] * scale[:, :, :t], axis=0) / total[:, :t]
    return jnp.concatenate([top + jnp.log(total), mean], axis=1)


LINES_X = [[x * NY + y for x in range(NX)] for y in range(NY)]
LINES_Y = [[x * NY + y for y in range(NY)] for x in range(NX)]


def by_core(first, second):
    return first + [[NX * NY + i for i in line] for line in second]


FIRST, LAST = by_core(LINES_X, LINES_Y), by_core(LINES_Y, LINES_X)


def spread_groups(x, axes, lines):
    copies = jnp.broadcast_to(x[None], (len(lines[0]),) + x.shape)
    return lax.all_to_all(copies, axes, 0, 0, axis_index_groups=lines)


def place_kernel(shifts, *refs):
    out = refs[-1]
    core = lax.axis_index("core")
    me = jnp.where(core == 0, lax.axis_index("y"), lax.axis_index("x"))
    for piece, shift in zip(refs, shifts):
        source = (me - shift) & (NX - 1)
        for j in range(NX):
            a = jnp.where(core == 0, j, source)
            b = jnp.where(core == 0, source, j)
            out[a, b] = piece[j]


def place(pieces, shifts, into=()):
    n = len(pieces)
    whole = pl.BlockSpec(memory_space=pltpu.VMEM)
    shape = (NX, NY) + pieces[0].shape[1:]
    return pl.pallas_call(
        functools.partial(place_kernel, shifts),
        out_shape=jax.ShapeDtypeStruct(shape, pieces[0].dtype),
        in_specs=[whole] * (n + len(into)),
        out_specs=whole,
        input_output_aliases={n: 0} if into else {},
        compiler_params=pltpu.CompilerParams(vmem_limit_bytes=4 * 1024 * 1024),
        name="place_blocks",
    )(*pieces, *(pltpu.with_memory_space_constraint(b, pltpu.VMEM) for b in into))


def per_device(student_hidden, teacher_hidden, student_head, teacher_head, route):
    core = lax.axis_index("core")
    x, y, z = lax.axis_index("x"), lax.axis_index("y"), lax.axis_index("z")
    feats = student_hidden.shape[1]
    rows = student_head.shape[0]
    groups = NZ * NC
    per_group = 2 * BLK
    half = NZ * BLK
    cols = 2 * half
    width = NX * NY * feats
    f32, bf16 = jnp.float32, jnp.bfloat16

    held = jnp.concatenate([student_hidden, teacher_hidden], axis=0)
    n_rows = held.shape[0]
    got = lax.all_gather(held, ("z", "core"))
    row = lax.broadcasted_iota(jnp.int32, (groups, n_rows), 1)
    group = lax.broadcasted_iota(jnp.int32, (groups, n_rows), 0)
    block = 2 * group + row // BLK
    for b in range(route.shape[1]):
        block = jnp.where((row - per_group) // BLK == b, route[:, b : b + 1], block)
    column = (block & 1) * half + (block >> 2) * BLK + row % BLK + jnp.where(row < per_group, 0, cols)
    mine = (block < 2 * groups) & (((block >> 1) & 1) == core)
    column = jnp.where(mine, column, -1)
    onehot = (column[:, :, None] == jnp.arange(2 * cols, dtype=jnp.int32)).astype(bf16)
    placed = lax.dot_general(
        got, onehot, (((0, 1), (0, 1)), ((), ())), preferred_element_type=f32
    ).astype(bf16)

    student_other = lax.ppermute(student_head, "core", SWAP)
    teacher_other = lax.ppermute(teacher_head, "core", SWAP)

    plane = ("core", "x", "y")
    both = jnp.stack([placed[:, :cols], placed[:, cols:]])
    once = spread_groups(both, plane, FIRST)
    student_1, teacher_1 = once[:, 0], once[:, 1]

    def pass_on(piece, k):
        return lax.ppermute(piece, plane, [(i[j], i[(j + k) % len(i)]) for i in LAST for j in range(len(i))])

    student_b, teacher_a = pass_on(student_1, 1), pass_on(teacher_1, 3)
    student_a, teacher_b = pass_on(student_1, 3), pass_on(teacher_1, 1)
    student_b, student_other = lax.optimization_barrier((student_b, student_other))
    teacher_a, teacher_other = lax.optimization_barrier((teacher_a, teacher_other))
    student_c, teacher_c = pass_on(student_b, 1), pass_on(teacher_a, 3)
    near_s = place((student_1, student_b, student_a), (0, 1, 3))
    near_t = place((teacher_1, teacher_b, teacher_a), (0, 1, 3))
    head_s = jnp.concatenate([student_head, student_other], axis=0)
    head_t = jnp.concatenate([teacher_head, teacher_other], axis=0)
    near_s, head_s = lax.optimization_barrier((near_s, head_s))
    near_t, head_t = lax.optimization_barrier((near_t, head_t))
    student_t = place((student_c,), (2,), (near_s,)).reshape(width, cols)
    teacher_t = place((teacher_c,), (2,), (near_t,)).reshape(width, cols)

    student_mate = lax.ppermute(student_t, "core", SWAP)

    ls = jnp.dot(head_s, student_t, preferred_element_type=f32)
    lt = jnp.dot(head_t, teacher_t, preferred_element_type=f32)
    source, block_weight = block_sources(route, groups, TASKS, BLK, groups * per_group)
    my_weight = lax.dynamic_index_in_dim(block_weight.reshape(NZ, NC, 2), core, 1, keepdims=False)
    my_weight = jnp.repeat(my_weight.T.reshape(-1), BLK)
    ms = jnp.max(ls, axis=0)
    mt = jnp.max(lt, axis=0)
    es = jnp.exp(ls - ms[None])
    et = jnp.exp(lt - mt[None])
    total_s, total_t = jnp.sum(es, axis=0), jnp.sum(et, axis=0)
    mean = jnp.sum(et * (lt - ls), axis=0) / total_t
    stats = jnp.concatenate([mt + jnp.log(total_t), ms + jnp.log(total_s), mean])[None]
    stats = merge(spread(stats, ("x", "y"), NX * NY), cols)
    stats = merge(spread(stats, "z", NZ), cols)[0]
    lse_t, lse_s = stats[:cols], stats[cols : 2 * cols]
    grad = (
        my_weight[None] * (jnp.exp(ls - lse_s[None]) - jnp.exp(lt - lse_t[None]))
    ).astype(bf16)

    grad_in = lax.all_gather(grad[rows:], "core")
    grad_in = lax.dynamic_index_in_dim(grad_in, 1 - core, 0, keepdims=False)
    nt = (((1,), (1,)), ((), ()))
    student_mate = lax.optimization_barrier(jnp.where(z >= 0, student_mate, -student_mate))
    head_grad = lax.dot_general(grad_in, student_mate, nt, preferred_element_type=f32)
    head_grad += lax.dot_general(grad[:rows], student_t, nt, preferred_element_type=f32)
    head_grad = head_grad.astype(bf16)
    own = lax.dynamic_index_in_dim(stats.reshape(6, NZ, BLK), z, 1, keepdims=False)
    own = own.reshape(3, per_group)
    loss = own[2] - own[0] + own[1]
    return head_grad, loss


def solution(mesh):
    mesh = Mesh(np.asarray(mesh.devices).reshape(NZ, NC, NX, NY), ("z", "core", "x", "y"))
    grp, voc = ("z", "core"), ("x", "y")
    return jax.shard_map(
        per_device,
        mesh=mesh,
        in_specs=(P(grp, voc), P(grp, voc), P(grp + voc, None), P(grp + voc, None), P()),
        out_specs=(P(grp + voc, None), P(grp)),
        check_vma=False,
    )
```
